1024 devices in a mesh: row: 64 (over z, y_lo, core), col: 16 (over y_hi, x).
Axes of the slice: x: 4, y: 8 (y_hi: 4, y_lo: 2; y = y_hi * 2 + y_lo), z: 16, core: 2. Of those that a mesh axis runs over, the one named last changes fastest.
Arguments:
- a_vals: bfloat16 [64, 128, 192, 192], P('row', 'col'), may hold values from -0.75 to 0.75
- a_rows: int32 [64, 128], P('row', 'col'), may hold values from 0 to 31, as said below
- a_cols: int32 [64, 128], P('row', 'col'), may hold values from 28 to 67, as said below
- a_count: int32 [64, 16], P('row', 'col'), may hold values from 1 to 8, as said below
- p_vals: bfloat16 [2048, 2, 192, 192], P(('row', 'col')), may hold values from -0.4375 to 0.4375
- p_cols: int32 [2048, 2], replicated, may hold values from 0 to 1, as said below
Outputs:
- galerkin: float32 [24576, 1344], P(('row', 'col'))
The draws below stay inside these ranges and needn't reach their ends.
Inputs may be any that keep to these rules, and one draw needn't show every extreme that they name: `a_count`: live blocks of each tile; at least one tile has 8. `a_rows`: slot s of a group lies in the 32 // 16 block rows of tile s // 8, from (s // 8) * (32 // 16) on. a_cols - 32 - a_rows lies between -4 and 4. The two entries of p_cols[i], in either order, are c = (i % 32) // 16 and a coarse block that differs from c by one.
All inputs are finite; a program needn't handle non-finite values.
Results may differ from the reference program's by a relative error of at most 0.0029.
Values may be sent and summed in bfloat16 or wider, within the bound.
A program may use at most 32 MiB of HBM per device.

```python
import jax
import jax.numpy as jnp
from jax import lax

KB = 192
KP = 2
HB = 4
BAND = 7
RB = 32
SLOTS = 8
CR = 2
GROUPS = 64
TILE = 128
NB = 2048
NC = 128
N_COL = 16


def slot_pattern(key):
    key_row = jax.random.fold_in(key, 21)
    key_offset = jax.random.fold_in(key, 22)
    share = RB // N_COL
    tiles = jnp.arange(TILE, dtype=jnp.int32) // SLOTS
    rows = tiles[None, :] * share + jax.random.randint(key_row, (GROUPS, TILE), 0, share)
    offsets = jax.random.randint(key_offset, (GROUPS, TILE), -HB, HB + 1)
    rows = rows.at[0, 0].set(0)
    offsets = offsets.at[0, 0].set(-HB)
    rows = rows.at[0, TILE - 1].set(RB - 1)
    offsets = offsets.at[0, TILE - 1].set(HB)
    rows = rows.at[GROUPS - 1, TILE - 2].set(RB - share)
    offsets = offsets.at[GROUPS - 1, TILE - 2].set(-HB)
    rows = rows.at[GROUPS - 1, TILE - 3].set(RB - share)
    offsets = offsets.at[GROUPS - 1, TILE - 3].set(-1)
    columns = RB + rows + offsets
    return (rows.astype(jnp.int32), columns.astype(jnp.int32))


def draw_a_rows(key, part):
    return slot_pattern(key)[0]


def draw_a_cols(key, part):
    return slot_pattern(key)[1]


def draw_p_cols(key, part):
    key_side = jax.random.fold_in(key, 31)
    key_order = jax.random.fold_in(key, 32)
    fine_rows = jnp.arange(NB, dtype=jnp.int32)
    first = fine_rows % RB // (RB // CR)
    side = jax.random.randint(key_side, (NB,), 0, 2) * 2 - 1
    second = first + side
    second = jnp.where(second < 0, first + 1, second)
    second = jnp.where(second > CR - 1, first - 1, second)
    flip = jax.random.randint(key_order, (NB,), 0, 2)
    left = jnp.where(flip == 1, second, first)
    right = jnp.where(flip == 1, first, second)
    return jnp.stack([left, right], axis=1).astype(jnp.int32)


def draw_a_count(key, part):
    key_first = jax.random.fold_in(key, 11)
    key_second = jax.random.fold_in(key, 12)
    key_place = jax.random.fold_in(key, 13)
    columns = TILE // SLOTS
    first_draw = jax.random.randint(key_first, (GROUPS, columns), 1, SLOTS + 1)
    second_draw = jax.random.randint(key_second, (GROUPS, columns), 1, SLOTS + 1)
    counts = jnp.minimum(first_draw, second_draw).reshape(-1)
    place = jax.random.randint(key_place, (), 0, GROUPS * columns)
    counts = counts.at[place].set(SLOTS)
    counts = counts.at[GROUPS * columns - 1].set(SLOTS)
    return counts.reshape(GROUPS, columns).astype(jnp.int32)


def steps_of(key, dims, split, low, top_value):
    def one(axis_at, blocks):
        draws = jax.random.uniform(jax.random.fold_in(jax.random.fold_in(key, 6), axis_at), (blocks,), jnp.float32, low / len(split), top_value / len(split))
        return jnp.repeat(jnp.exp(draws), dims[axis_at] // blocks).reshape((-1,) + (1,) * (len(dims) - axis_at - 1))

    level = one(*split[0])
    for cut in split[1:]:
        level = level * one(*cut)
    return level


def noise(key, extent, width, bound, pieces=(), kind=jnp.bfloat16):
    drawn = jax.random.normal(key, extent, jnp.float32) * width
    if len(pieces) > 0:
        drawn = steps_of(key, extent, pieces, -0.22, 0.18) * drawn
    return jnp.clip(drawn, min=-bound, max=bound).astype(kind)


def setup_inputs(seed: int = 0) -> dict:
    key_list = jax.random.split(jax.random.key(seed), 7)
    return {
        "a_vals": noise(key_list[0], (GROUPS, TILE, KB, KB), 0.125, 0.75, ((0, 64), (1, 16))),
        "a_rows": draw_a_rows(jax.random.fold_in(key_list[6], 71), 0),
        "a_cols": draw_a_cols(jax.random.fold_in(key_list[6], 71), 0),
        "a_count": draw_a_count(jax.random.fold_in(key_list[6], 71), 0),
        "p_vals": noise(key_list[4], (NB, KP, KB, KB), KB ** -0.5, 0.4375, ((0, 1024),)),
        "p_cols": draw_p_cols(jax.random.fold_in(key_list[6], 71), 0),
    }


def reference(a_vals, a_rows, a_cols, a_count, p_vals, p_cols):
    zeros_rim = jnp.zeros((HB,) + p_vals.shape[1:], p_vals.dtype)
    padded_vals = jnp.concatenate([zeros_rim, p_vals, zeros_rim], axis=0)

    def one_group(group_index):
        blocks = a_vals[group_index].astype(jnp.float32)
        left_ids = a_rows[group_index]
        right_ids = a_cols[group_index]
        counts = a_count[group_index]
        slot_ids = jnp.arange(TILE, dtype=jnp.int32)
        slot_live = (slot_ids % SLOTS < counts[slot_ids // SLOTS]).astype(jnp.float32)
        left_global = (group_index * RB + left_ids).astype(jnp.int32)
        right_global = ((group_index - 1) * RB + right_ids).astype(jnp.int32)
        left_rows = p_vals[left_global].astype(jnp.float32)
        right_rows = padded_vals[right_global + HB].astype(jnp.float32)
        left_coarse = p_cols[left_global]
        right_coarse = (right_ids // RB - 1)[:, None] * CR + p_cols[jnp.clip(right_global, 0, NB - 1)]
        offset = right_coarse[:, None, :] - left_coarse[:, :, None] + BAND // 2
        left_hot = (left_coarse[..., None] == jnp.arange(CR, dtype=jnp.int32)).astype(jnp.float32)
        left_hot = left_hot * slot_live[:, None, None]
        offset_hot = (offset[..., None] == jnp.arange(BAND, dtype=jnp.int32)).astype(jnp.float32)
        weights = jnp.einsum('sua,sutd->sutad', left_hot, offset_hot)
        weights = weights.reshape(TILE, KP, KP, CR * BAND)
        product = jnp.einsum('sxy,skyz->skxz', blocks, right_rows).astype(jnp.bfloat16)
        triple = jnp.einsum('suxw,stxz->sutwz', left_rows, product.astype(jnp.float32))
        band = jnp.einsum('sutq,sutwz->qwz', weights, triple, precision=lax.Precision.HIGHEST)
        band = jnp.transpose(band.reshape(CR, BAND, KB, KB), (0, 2, 1, 3))
        return band.reshape(CR * KB, BAND * KB)

    bands = lax.map(one_group, jnp.arange(GROUPS, dtype=jnp.int32))
    return bands.reshape(NC * KB, BAND * KB)
```

```python
import functools

import jax
import jax.numpy as jnp
from jax import lax
from jax.experimental import pallas as pl
from jax.experimental.pallas import tpu as pltpu
from jax.sharding import PartitionSpec as P

HB = 4
RB = 32
CR = 2
LANES = 128
CHUNKS = 3
MESH = pl.DeviceIdType.MESH
HALO = (1, -1, 2, -2)


def kernel(
    a_hbm, rows_hbm, cols_hbm, count_hbm, p_hbm, pc_hbm, out_ref,
    a_buf, p_buf, rows_s, cols_s, count_s, pc_s,
    own, halo0, halo1, halo2, stack, left, side_left, prod,
    mine, got0, got1, got2, side_mine, side_got0, side_got1, side_got2,
    load_sem, halo_send, halo_recv, band_send, band_recv, side_send, side_recv,
):
    rows_n, cols_n = lax.axis_size("row"), lax.axis_size("col")
    r, t = lax.axis_index("row"), lax.axis_index("col")
    slots, size = a_buf.shape[0], a_buf.shape[1]
    share = p_buf.shape[0]
    half = size - LANES
    piece = CR * size // cols_n
    halos, gots, side_gots = (halo0, halo1, halo2), (got0, got1, got2), (side_got0, side_got1, side_got2)
    first_row = r * RB + t * share
    aligned = pl.multiple_of(first_row // LANES * LANES, LANES)

    def shifted(by):
        flat = lax.rem(r * cols_n + t + by + rows_n * cols_n, rows_n * cols_n)
        return flat // cols_n, lax.rem(flat, cols_n)

    def peer(by):
        return r, lax.rem(t + by, cols_n)

    loads = [
        pltpu.make_async_copy(p_hbm, p_buf, load_sem.at[0]),
        pltpu.make_async_copy(pc_hbm.at[:, pl.ds(aligned, LANES)], pc_s, load_sem.at[1]),
        pltpu.make_async_copy(a_hbm.at[0], a_buf, load_sem.at[2]),
        pltpu.make_async_copy(rows_hbm, rows_s, load_sem.at[3]),
        pltpu.make_async_copy(cols_hbm, cols_s, load_sem.at[4]),
        pltpu.make_async_copy(count_hbm, count_s, load_sem.at[5]),
    ]
    for load in loads:
        load.start()

    barrier = pltpu.get_barrier_semaphore()
    for by in HALO:
        pl.semaphore_signal(barrier, inc=1, device_id=shifted(by), device_id_type=MESH)
    for by in range(1, cols_n):
        pl.semaphore_signal(barrier, inc=1, device_id=peer(by), device_id_type=MESH)

    loads[0].wait()
    loads[1].wait()
    for k in range(share):
        swap = jnp.clip(pc_s[0, first_row - aligned + k], 0, 1)
        low = p_buf[k, swap]
        high = p_buf[k, 1 - swap]
        parts = (low[:, :LANES], high[:, :LANES], jnp.concatenate([low[:, LANES:], high[:, LANES:]], axis=1))
        for c in range(CHUNKS):
            own[c, k] = parts[c]
            halos[c][HB + k] = parts[c]

    pl.semaphore_wait(barrier, len(HALO) + cols_n - 1)

    def halo_copy(c, n):
        by = HALO[n]
        return pltpu.make_async_remote_copy(
            src_ref=own.at[c],
            dst_ref=halos[c].at[pl.ds(HB - share * by, share)],
            send_sem=halo_send.at[c, n],
            recv_sem=halo_recv.at[c, n],
            device_id=shifted(by),
            device_id_type=MESH,
        )

    for c in range(CHUNKS):
        for n in range(len(HALO)):
            halo_copy(c, n).start()

    for load in loads[2:]:
        load.wait()
    edge = (t < 2) | (t >= cols_n - 2)
    total_rows = rows_n * RB
    count = count_s[0, 0]
    picks = []
    for s in range(slots):
        column = cols_s[0, s]
        row = (r - 1) * RB + column
        live = (count > s) & (row >= 0) & (row < total_rows)
        centre = (column >= RB) & (column < 2 * RB)
        picks.append(jnp.clip(column - RB - t * share + HB, 0, halo0.shape[0] - 1))
        line = jnp.clip(rows_s[0, s] - t * share, 0, share - 1)
        for c in range(CHUNKS):
            value = own[c, line]
            zero = jnp.zeros_like(value)
            stack[c, s * size : (s + 1) * size, :] = jnp.where(live & centre, value, zero)

    def turn(into):
        flips = [stack[c].T for c in range(CHUNKS)]
        into[0:LANES, :] = flips[0]
        into[LANES:size, :] = flips[2][:half]
        into[size : size + LANES, :] = flips[1]
        into[size + LANES :, :] = flips[2][half:]

    turn(left)

    @pl.when(edge)
    def _():
        for s in range(slots):
            column = cols_s[0, s]
            row = (r - 1) * RB + column
            live = (count > s) & (row >= 0) & (row < total_rows)
            outside = (column < RB) | (column >= 2 * RB)
            line = jnp.clip(rows_s[0, s] - t * share, 0, share - 1)
            for c in range(CHUNKS):
                value = own[c, line]
                zero = jnp.zeros_like(value)
                stack[c, s * size : (s + 1) * size, :] = jnp.where(live & outside, value, zero)
        turn(side_left)

    side_slot = jnp.where(t < 2, t, t - cols_n + 4)

    def pieces(value):
        value = value.reshape(cols_n, piece, LANES)
        pad = jnp.zeros((cols_n, mine.shape[2] - piece, LANES), value.dtype)
        return jnp.concatenate([value, pad], axis=1).astype(mine.dtype)

    def band_copy(c, by):
        return pltpu.make_async_remote_copy(
            src_ref=mine.at[c, lax.rem(t + by, cols_n)],
            dst_ref=gots[c].at[t],
            send_sem=band_send.at[c],
            recv_sem=band_recv.at[c],
            device_id=peer(by),
            device_id_type=MESH,
        )

    def side_copy(c, by):
        return pltpu.make_async_remote_copy(
            src_ref=side_mine.at[c, lax.rem(t + by, cols_n)],
            dst_ref=side_gots[c].at[side_slot],
            send_sem=side_send.at[c],
            recv_sem=side_recv.at[c],
            device_id=peer(by),
            device_id_type=MESH,
        )

    for c in range(CHUNKS):
        for n in range(len(HALO)):
            halo_copy(c, n).wait_recv()
        for s in range(slots):
            value = jnp.dot(a_buf[s], halos[c][picks[s]], preferred_element_type=jnp.float32)
            prod[s * size : (s + 1) * size, :] = value.astype(prod.dtype)
        mine[c] = pieces(jnp.dot(left[...], prod[...], preferred_element_type=jnp.float32))
        for by in range(1, cols_n):
            band_copy(c, by).start()
        gots[c][t] = mine[c, t]

        @pl.when(edge)
        def _():
            side_mine[c] = pieces(jnp.dot(side_left[...], prod[...], preferred_element_type=jnp.float32))
            for by in range(1, cols_n):
                side_copy(c, by).start()
            side_gots[c][side_slot] = side_mine[c, t]

    for c in range(CHUNKS):
        for n in range(len(HALO)):
            halo_copy(c, n).wait_send()

    sums = []
    for c in range(CHUNKS):
        everyone = pl.ds(0, cols_n - 1)
        pltpu.make_async_copy(gots[c].at[everyone], gots[c].at[everyone], band_recv.at[c]).wait()

        @pl.when(edge)
        def _():
            pltpu.make_async_copy(side_gots[c].at[pl.ds(0, 3)], side_gots[c].at[pl.ds(0, 3)], side_recv.at[c]).wait()

        @pl.when(jnp.logical_not(edge))
        def _():
            pltpu.make_async_copy(side_gots[c], side_gots[c], side_recv.at[c]).wait()

        centre = jnp.sum(gots[c][...].astype(jnp.float32), axis=0)[:piece]
        sides = side_gots[c][...].astype(jnp.float32)
        sums.append(((sides[0] + sides[1])[:piece], centre, (sides[2] + sides[3])[:piece]))

    for c in range(CHUNKS):
        everyone = pl.ds(0, cols_n - 1)
        pltpu.make_async_copy(mine.at[c, everyone], mine.at[c, everyone], band_send.at[c]).wait()

        @pl.when(edge)
        def _():
            pltpu.make_async_copy(side_mine.at[c, everyone], side_mine.at[c, everyone], side_send.at[c]).wait()

    blocks = []
    for j in range(3):
        first, second, mixed = sums[0][j], sums[1][j], sums[2][j]
        blocks += [first, mixed[:, :half], second, mixed[:, half:]]
    empty = jnp.zeros((piece, size), jnp.float32)

    @pl.when(t < cols_n // CR)
    def _():
        out_ref[...] = jnp.concatenate([empty] + blocks, axis=1)

    @pl.when(t >= cols_n // CR)
    def _():
        out_ref[...] = jnp.concatenate(blocks + [empty], axis=1)


def local(a_vals, a_rows, a_cols, a_count, p_vals, p_cols):
    slots, size = a_vals.shape[1], a_vals.shape[2]
    share = p_vals.shape[0]
    cols_n = lax.axis_size("col")
    piece = CR * size // cols_n
    padded = -(-piece // 16) * 16
    width = share + 2 * HB
    kind = p_vals.dtype
    anywhere = pl.BlockSpec(memory_space=pltpu.HBM)
    halo = pltpu.VMEM((width, size, LANES), kind)
    got = pltpu.VMEM((cols_n, padded, LANES), kind)
    side_got = pltpu.VMEM((4, padded, LANES), kind)
    return pl.pallas_call(
        kernel,
        out_shape=jax.ShapeDtypeStruct((piece, 7 * size), jnp.float32),
        in_specs=[anywhere] * 6,
        out_specs=pl.BlockSpec(memory_space=pltpu.VMEM),
        scratch_shapes=[
            pltpu.VMEM((slots, size, size), kind),
            pltpu.VMEM((share, 2, size, size), kind),
            pltpu.SMEM((1, slots), jnp.int32),
            pltpu.SMEM((1, slots), jnp.int32),
            pltpu.SMEM((1, 1), jnp.int32),
            pltpu.SMEM((2, LANES), jnp.int32),
            pltpu.VMEM((CHUNKS, share, size, LANES), kind),
            halo, halo, halo,
            pltpu.VMEM((CHUNKS, slots * size, LANES), kind),
            pltpu.VMEM((CR * size, slots * size), kind),
            pltpu.VMEM((CR * size, slots * size), kind),
            pltpu.VMEM((slots * size, LANES), kind),
            pltpu.VMEM((CHUNKS, cols_n, padded, LANES), kind),
            got, got, got,
            pltpu.VMEM((CHUNKS, cols_n, padded, LANES), kind),
            side_got, side_got, side_got,
            pltpu.SemaphoreType.DMA((6,)),
            pltpu.SemaphoreType.DMA((CHUNKS, len(HALO))),
            pltpu.SemaphoreType.DMA((CHUNKS, len(HALO))),
            pltpu.SemaphoreType.DMA((CHUNKS,)),
            pltpu.SemaphoreType.DMA((CHUNKS,)),
            pltpu.SemaphoreType.DMA((CHUNKS,)),
            pltpu.SemaphoreType.DMA((CHUNKS,)),
        ],
        compiler_params=pltpu.CompilerParams(
            collective_id=0, has_side_effects=True, vmem_limit_bytes=62 * 2**20
        ),
        name="galerkin",
    )(a_vals, a_rows, a_cols, a_count, p_vals, p_cols.T)


def solution(mesh):
    placed = (
        P("row", "col", None, None),
        P("row", "col"),
        P("row", "col"),
        P("row", "col"),
        P(("row", "col"), None, None, None),
        P(),
    )
    return jax.shard_map(
        local, mesh=mesh, in_specs=placed, out_specs=P(("row", "col"), None), check_vma=False
    )
```

```python
import functools

import jax
import jax.numpy as jnp
from jax import lax
from jax.experimental import pallas as pl
from jax.experimental.pallas import tpu as pltpu
from jax.sharding import PartitionSpec as P

HB = 4
RB = 32
CR = 2
LANES = 128
CHUNKS = 3
MESH = pl.DeviceIdType.MESH
SPAN = 4


def kernel(
    a_hbm, rows_hbm, cols_hbm, count_hbm, p_hbm, pc_hbm, out_ref,
    a_buf, p_buf, rows_s, cols_s, count_s, pc_s,
    own, halo0, halo1, halo2, relay, stack, left, side_left, prod,
    mine, got0, got1, got2, side_mine, side_got0, side_got1, side_got2,
    part, lined0, lined1, lined2, side_part, side_lined0, side_lined1, side_lined2,
    load_sem, halo_send, halo_recv, relay_send, relay_recv, skip_send,
    band_send, band_recv, side_send, side_recv, line_send, line_recv, side_line_send, side_line_recv,
):
    rows_n, cols_n = lax.axis_size("row"), lax.axis_size("col")
    r, t = lax.axis_index("row"), lax.axis_index("col")
    slots, size = a_buf.shape[0], a_buf.shape[1]
    share = p_buf.shape[0]
    half = size - LANES
    piece = CR * size // cols_n
    lined, side_lined = (lined0, lined1, lined2), (side_lined0, side_lined1, side_lined2)
    halos, gots, side_gots = (halo0, halo1, halo2), (got0, got1, got2), (side_got0, side_got1, side_got2)
    first_row = r * RB + t * share
    aligned = pl.multiple_of(first_row // LANES * LANES, LANES)

    def shifted(by):
        flat = lax.rem(r * cols_n + t + by + rows_n * cols_n, rows_n * cols_n)
        return flat // cols_n, lax.rem(flat, cols_n)

    lines = cols_n // SPAN
    place, line_of = lax.rem(t, SPAN), t // SPAN
    first, last = place == 0, place == SPAN - 1

    def beside(by):
        return r, line_of * SPAN + lax.rem(place + by, SPAN)

    def above(by):
        return r, lax.rem(t + by * SPAN, cols_n)

    loads = [
        pltpu.make_async_copy(p_hbm, p_buf, load_sem.at[0]),
        pltpu.make_async_copy(pc_hbm.at[:, pl.ds(aligned, LANES)], pc_s, load_sem.at[1]),
        pltpu.make_async_copy(a_hbm.at[0], a_buf, load_sem.at[2]),
        pltpu.make_async_copy(rows_hbm, rows_s, load_sem.at[3]),
        pltpu.make_async_copy(cols_hbm, cols_s, load_sem.at[4]),
        pltpu.make_async_copy(count_hbm, count_s, load_sem.at[5]),
    ]
    for load in loads:
        load.start()

    barrier = pltpu.get_barrier_semaphore()
    friends = [shifted(by) for by in (1, -1, 2, -2, SPAN, -SPAN)]
    friends += [beside(by) for by in range(1, SPAN)] + [above(by) for by in range(1, lines)]
    for friend in friends:
        pl.semaphore_signal(barrier, inc=1, device_id=friend, device_id_type=MESH)

    loads[0].wait()
    loads[1].wait()
    for k in range(share):
        swap = jnp.clip(pc_s[0, first_row - aligned + k], 0, 1)
        low = p_buf[k, swap]
        high = p_buf[k, 1 - swap]
        parts = (low[:, :LANES], high[:, :LANES], jnp.concatenate([low[:, LANES:], high[:, LANES:]], axis=1))
        for c in range(CHUNKS):
            own[c, k] = parts[c]
            halos[c][HB + k] = parts[c]

    pl.semaphore_wait(barrier, len(friends))

    def halo_copy(source, target, device, sent, landed):
        return pltpu.make_async_remote_copy(
            src_ref=source,
            dst_ref=target,
            send_sem=sent,
            recv_sem=landed,
            device_id=device,
            device_id_type=MESH,
        )

    def rows_at(c, start):
        return halos[c].at[pl.ds(start, share)]

    def near_copy(c, n):
        by = 1 - 2 * n
        return halo_copy(
            own.at[c], rows_at(c, HB - share * by), shifted(by), halo_send.at[c, n], halo_recv.at[c, n]
        )

    def far_copy(c, n):
        by = 1 - 2 * n
        source, target = rows_at(c, HB - share * by), rows_at(c, HB - 2 * share * by)
        return halo_copy(source, target, shifted(by), halo_send.at[c, 2 + n], halo_recv.at[c, 2 + n])

    def to_relay(c, n):
        by = 1 - 2 * n
        across = r, t - (SPAN - 1) * by
        source = rows_at(c, HB - share * by)
        return halo_copy(source, relay.at[c], across, halo_send.at[c, 2 + n], relay_recv.at[c])

    def from_relay(c, n):
        by = 1 - 2 * n
        target = rows_at(c, HB - 2 * share * by)
        return halo_copy(relay.at[c], target, shifted(SPAN * by), relay_send.at[c], halo_recv.at[c, 2 + n])

    def skip_copy(n):
        by = 1 - 2 * n
        target = rows_at(0, HB - 2 * share * by)
        return halo_copy(own.at[0], target, shifted(2 * by), skip_send, halo_recv.at[0, 2 + n])

    def pass_on(c):
        for n, turning in ((0, last), (1, first)):
            near_copy(c, n).wait_recv()

            if c > 0:

                @pl.when(turning)
                def _():
                    to_relay(c, n).start()

            @pl.when(jnp.logical_not(turning))
            def _():
                far_copy(c, n).start()

    def pass_relay(c):
        for n, turning in ((0, first), (1, last)):

            @pl.when(turning)
            def _():
                to_relay(c, n).wait_recv()
                from_relay(c, n).start()

    skips = (place == SPAN - 2, place == 1)
    for c in range(2):
        for n in range(2):
            near_copy(c, n).start()

            if c == 0:

                @pl.when(skips[n])
                def _():
                    skip_copy(n).start()

    for load in loads[2:]:
        load.wait()
    edge = (t < 2) | (t >= cols_n - 2)
    total_rows = rows_n * RB
    count = count_s[0, 0]
    picks = []
    for s in range(slots):
        column = cols_s[0, s]
        row = (r - 1) * RB + column
        live = (count > s) & (row >= 0) & (row < total_rows)
        centre = (column >= RB) & (column < 2 * RB)
        picks.append(jnp.clip(column - RB - t * share + HB, 0, halo0.shape[0] - 1))
        line = jnp.clip(rows_s[0, s] - t * share, 0, share - 1)
        for c in range(CHUNKS):
            value = own[c, line]
            zero = jnp.zeros_like(value)
            stack[c, s * size : (s + 1) * size, :] = jnp.where(live & centre, value, zero)

    def turn(into):
        flips = [stack[c].T for c in range(CHUNKS)]
        into[0:LANES, :] = flips[0]
        into[LANES:size, :] = flips[2][:half]
        into[size : size + LANES, :] = flips[1]
        into[size + LANES :, :] = flips[2][half:]

    pass_on(0)
    for n in range(2):
        near_copy(2, n).start()
    turn(left)
    pass_on(1)

    @pl.when(edge)
    def _():
        for s in range(slots):
            column = cols_s[0, s]
            row = (r - 1) * RB + column
            live = (count > s) & (row >= 0) & (row < total_rows)
            outside = (column < RB) | (column >= 2 * RB)
            line = jnp.clip(rows_s[0, s] - t * share, 0, share - 1)
            for c in range(CHUNKS):
                value = own[c, line]
                zero = jnp.zeros_like(value)
                stack[c, s * size : (s + 1) * size, :] = jnp.where(live & outside, value, zero)
        turn(side_left)

    pass_relay(1)
    pass_on(2)
    def pieces(value):
        value = value.reshape(lines, SPAN, piece, LANES)
        value = jnp.stack([value[:, k] for k in range(SPAN)])
        return value.reshape(SPAN, lines * piece, LANES).astype(mine.dtype)

    def band_copy(c, by):
        device = beside(by)
        return pltpu.make_async_remote_copy(
            src_ref=mine.at[c, lax.rem(place + by, SPAN)],
            dst_ref=gots[c].at[place],
            send_sem=band_send.at[c],
            recv_sem=band_recv.at[c],
            device_id=device,
            device_id_type=MESH,
        )

    def side_copy(c, by):
        return pltpu.make_async_remote_copy(
            src_ref=side_mine.at[c, lax.rem(place + by, SPAN)],
            dst_ref=side_gots[c].at[lax.rem(t, 2)],
            send_sem=side_send.at[c],
            recv_sem=side_recv.at[c],
            device_id=beside(by),
            device_id_type=MESH,
        )

    def line_copy(c, by):
        return pltpu.make_async_remote_copy(
            src_ref=part.at[c, lax.rem(line_of + by, lines)],
            dst_ref=lined[c].at[line_of],
            send_sem=line_send.at[c],
            recv_sem=line_recv.at[c],
            device_id=above(by),
            device_id_type=MESH,
        )

    def side_line_copy(c, by):
        return pltpu.make_async_remote_copy(
            src_ref=side_part.at[c, lax.rem(line_of + by, lines)],
            dst_ref=side_lined[c].at[line_of // (lines - 1)],
            send_sem=side_line_send.at[c],
            recv_sem=side_line_recv.at[c, line_of // (lines - 1)],
            device_id=above(by),
            device_id_type=MESH,
        )

    def landed(ref, count, sem):
        some = ref.at[pl.ds(0, count)]
        pltpu.make_async_copy(some, some, sem).wait()

    outer = (line_of == 0) | (line_of == lines - 1)

    def work(c):
        for n in range(2):
            far_copy(c, n).wait_recv()
        for s in range(slots):
            value = jnp.dot(a_buf[s], halos[c][picks[s]], preferred_element_type=jnp.float32)
            prod[s * size : (s + 1) * size, :] = value.astype(prod.dtype)
        mine[c] = pieces(jnp.dot(left[...], prod[...], preferred_element_type=jnp.float32))
        for by in range(1, SPAN):
            band_copy(c, by).start()
        gots[c][place] = mine[c, place]

        @pl.when(edge)
        def _():
            side_mine[c] = pieces(jnp.dot(side_left[...], prod[...], preferred_element_type=jnp.float32))
            for by in range(1, SPAN):
                side_copy(c, by).start()
            side_gots[c][lax.rem(t, 2)] = side_mine[c, place]

    def hand_on(c):
        landed(gots[c], SPAN - 1, band_recv.at[c])
        total = jnp.sum(gots[c][...].astype(jnp.float32), axis=0).reshape(lines, piece, LANES)
        part[c] = total
        for by in range(1, lines):
            line_copy(c, by).start()
        lined[c][line_of] = part[c, line_of]

        @pl.when(outer)
        def _():
            @pl.when(edge)
            def _():
                landed(side_gots[c], 1, side_recv.at[c])

            @pl.when(jnp.logical_not(edge))
            def _():
                landed(side_gots[c], 2, side_recv.at[c])

            sides = side_gots[c][...].astype(jnp.float32)
            side_part[c] = (sides[0] + sides[1]).reshape(lines, piece, LANES)
            for by in range(1, lines):
                side_line_copy(c, by).start()
            side_lined[c][line_of // (lines - 1)] = side_part[c, line_of]

    work(0)
    pass_relay(2)
    work(1)
    hand_on(0)
    work(2)
    hand_on(1)
    hand_on(2)
    for c in range(CHUNKS):
        for n in range(2):
            near_copy(c, n).wait_send()
            if c > 0:
                far_copy(c, n).wait_send()

                @pl.when((first, last)[n])
                def _():
                    from_relay(c, n).wait_send()

            else:

                @pl.when(jnp.logical_not((last, first)[n]))
                def _():
                    far_copy(c, n).wait_send()

                @pl.when(skips[n])
                def _():
                    skip_copy(n).wait_send()

    sums = []
    for c in range(CHUNKS):
        landed(lined[c], lines - 1, line_recv.at[c])
        for k in range(2):

            @pl.when(line_of != k * (lines - 1))
            def _():
                landed(side_lined[c], 1, side_line_recv.at[c, k])

        sums.append((side_lined[c][0], jnp.sum(lined[c][...], axis=0), side_lined[c][1]))

    for c in range(CHUNKS):
        landed(mine.at[c], SPAN - 1, band_send.at[c])
        landed(part.at[c], lines - 1, line_send.at[c])

        @pl.when(edge)
        def _():
            landed(side_mine.at[c], SPAN - 1, side_send.at[c])

        @pl.when(outer)
        def _():
            landed(side_part.at[c], lines - 1, side_line_send.at[c])

    blocks = []
    for j in range(3):
        low, high, mixed = sums[0][j], sums[1][j], sums[2][j]
        blocks += [low, mixed[:, :half], high, mixed[:, half:]]
    empty = jnp.zeros((piece, size), jnp.float32)

    @pl.when(t < cols_n // CR)
    def _():
        out_ref[...] = jnp.concatenate([empty] + blocks, axis=1)

    @pl.when(t >= cols_n // CR)
    def _():
        out_ref[...] = jnp.concatenate(blocks + [empty], axis=1)


def local(a_vals, a_rows, a_cols, a_count, p_vals, p_cols):
    slots, size = a_vals.shape[1], a_vals.shape[2]
    share = p_vals.shape[0]
    cols_n = lax.axis_size("col")
    piece = CR * size // cols_n
    lines = cols_n // SPAN
    width = share + 2 * HB
    kind = p_vals.dtype
    anywhere = pl.BlockSpec(memory_space=pltpu.HBM)
    halo = pltpu.VMEM((width, size, LANES), kind)
    got = pltpu.VMEM((SPAN, lines * piece, LANES), kind)
    side_got = pltpu.VMEM((2, lines * piece, LANES), kind)
    lined = pltpu.VMEM((lines, piece, LANES), jnp.float32)
    side_lined = pltpu.VMEM((2, piece, LANES), jnp.float32)
    return pl.pallas_call(
        kernel,
        out_shape=jax.ShapeDtypeStruct((piece, 7 * size), jnp.float32),
        in_specs=[anywhere] * 6,
        out_specs=pl.BlockSpec(memory_space=pltpu.VMEM),
        scratch_shapes=[
            pltpu.VMEM((slots, size, size), kind),
            pltpu.VMEM((share, 2, size, size), kind),
            pltpu.SMEM((1, slots), jnp.int32),
            pltpu.SMEM((1, slots), jnp.int32),
            pltpu.SMEM((1, 1), jnp.int32),
            pltpu.SMEM((2, LANES), jnp.int32),
            pltpu.VMEM((CHUNKS, share, size, LANES), kind),
            halo, halo, halo,
            pltpu.VMEM((CHUNKS, share, size, LANES), kind),
            pltpu.VMEM((CHUNKS, slots * size, LANES), kind),
            pltpu.VMEM((CR * size, slots * size), kind),
            pltpu.VMEM((CR * size, slots * size), kind),
            pltpu.VMEM((slots * size, LANES), kind),
            pltpu.VMEM((CHUNKS, SPAN, lines * piece, LANES), kind),
            got, got, got,
            pltpu.VMEM((CHUNKS, SPAN, lines * piece, LANES), kind),
            side_got, side_got, side_got,
            pltpu.VMEM((CHUNKS, lines, piece, LANES), jnp.float32),
            lined, lined, lined,
            pltpu.VMEM((CHUNKS, lines, piece, LANES), jnp.float32),
            side_lined, side_lined, side_lined,
            pltpu.SemaphoreType.DMA((6,)),
            pltpu.SemaphoreType.DMA((CHUNKS, 4)),
            pltpu.SemaphoreType.DMA((CHUNKS, 4)),
            pltpu.SemaphoreType.DMA((CHUNKS,)),
            pltpu.SemaphoreType.DMA((CHUNKS,)),
            pltpu.SemaphoreType.DMA,
        ]
        + [pltpu.SemaphoreType.DMA((CHUNKS,))] * 7
        + [pltpu.SemaphoreType.DMA((CHUNKS, 2))],
        compiler_params=pltpu.CompilerParams(
            collective_id=0, has_side_effects=True, vmem_limit_bytes=62 * 2**20
        ),
        name="galerkin",
    )(a_vals, a_rows, a_cols, a_count, p_vals, p_cols.T)


def solution(mesh):
    placed = (
        P("row", "col", None, None),
        P("row", "col"),
        P("row", "col"),
        P("row", "col"),
        P(("row", "col"), None, None, None),
        P(),
    )
    return jax.shard_map(
        local, mesh=mesh, in_specs=placed, out_specs=P(("row", "col"), None), check_vma=False
    )
```

```python
import functools

import jax
import jax.numpy as jnp
from jax import lax
from jax.experimental import pallas as pl
from jax.experimental.pallas import tpu as pltpu
from jax.sharding import PartitionSpec as P

HB = 4
RB = 32
CR = 2
LANES = 128
CHUNKS = 3
MESH = pl.DeviceIdType.MESH
SPAN = 4


def kernel(
    a_hbm, rows_hbm, cols_hbm, count_hbm, p_hbm, pc_hbm, out_ref,
    a_buf, p_buf, rows_s, cols_s, count_s, pc_s,
    own, halo0, halo1, halo2, relay, stack, left, side_left, prod,
    mine, got0, got1, got2, side_mine, side_got0, side_got1, side_got2,
    part, lined0, lined1, lined2, side_part, side_lined0, side_lined1, side_lined2,
    load_sem, halo_send, halo_recv, relay_send, relay_recv, skip_send,
    band_send, band_recv, side_send, side_recv, line_send, line_recv, side_line_send, side_line_recv,
):
    rows_n, cols_n = lax.axis_size("row"), lax.axis_size("col")
    r, t = lax.axis_index("row"), lax.axis_index("col")
    slots, size = a_buf.shape[0], a_buf.shape[1]
    share = p_buf.shape[0]
    half = size - LANES
    piece = CR * size // cols_n
    lined, side_lined = (lined0, lined1, lined2), (side_lined0, side_lined1, side_lined2)
    halos, gots, side_gots = (halo0, halo1, halo2), (got0, got1, got2), (side_got0, side_got1, side_got2)
    first_row = r * RB + t * share
    aligned = pl.multiple_of(first_row // LANES * LANES, LANES)

    flat = r * cols_n + t
    tiles = rows_n * cols_n

    def within(by):
        return (flat + by >= 0) & (flat + by < tiles)

    def shifted(by):
        other = lax.rem(flat + by + tiles, tiles)
        return other // cols_n, lax.rem(other, cols_n)

    lines = cols_n // SPAN
    place, line_of = lax.rem(t, SPAN), t // SPAN
    first, last = place == 0, place == SPAN - 1

    def beside(by):
        return r, line_of * SPAN + lax.rem(place + by, SPAN)

    def above(by):
        return r, lax.rem(t + by * SPAN, cols_n)

    loads = [
        pltpu.make_async_copy(p_hbm, p_buf, load_sem.at[0]),
        pltpu.make_async_copy(pc_hbm.at[:, pl.ds(aligned, LANES)], pc_s, load_sem.at[1]),
        pltpu.make_async_copy(a_hbm.at[0], a_buf, load_sem.at[2]),
        pltpu.make_async_copy(rows_hbm, rows_s, load_sem.at[3]),
        pltpu.make_async_copy(cols_hbm, cols_s, load_sem.at[4]),
        pltpu.make_async_copy(count_hbm, count_s, load_sem.at[5]),
    ]
    for load in loads:
        load.start()

    barrier = pltpu.get_barrier_semaphore()
    friends = [beside(by) for by in range(1, SPAN)] + [above(by) for by in range(1, lines)]
    for friend in friends:
        pl.semaphore_signal(barrier, inc=1, device_id=friend, device_id_type=MESH)
    expected = jnp.int32(len(friends))
    for by in (1, -1, 2, -2, SPAN, -SPAN):
        expected += within(by).astype(jnp.int32)

        @pl.when(within(by))
        def _():
            pl.semaphore_signal(barrier, inc=1, device_id=shifted(by), device_id_type=MESH)

    loads[0].wait()
    loads[1].wait()
    for k in range(share):
        swap = jnp.clip(pc_s[0, first_row - aligned + k], 0, 1)
        low = p_buf[k, swap]
        high = p_buf[k, 1 - swap]
        parts = (low[:, :LANES], high[:, :LANES], jnp.concatenate([low[:, LANES:], high[:, LANES:]], axis=1))
        for c in range(CHUNKS):
            own[c, k] = parts[c]
            halos[c][HB + k] = parts[c]

    for n in range(2):
        by = 1 - 2 * n
        for far in (1, 2):

            @pl.when(jnp.logical_not(within(-far * by)))
            def _():
                for c in range(CHUNKS):
                    empty_rows = jnp.zeros((share, size, LANES), halos[c].dtype)
                    halos[c][HB - far * share * by : HB - far * share * by + share] = empty_rows

    pl.semaphore_wait(barrier, expected)

    def halo_copy(source, target, device, sent, landed):
        return pltpu.make_async_remote_copy(
            src_ref=source,
            dst_ref=target,
            send_sem=sent,
            recv_sem=landed,
            device_id=device,
            device_id_type=MESH,
        )

    def rows_at(c, start):
        return halos[c].at[pl.ds(start, share)]

    def near_copy(c, n):
        by = 1 - 2 * n
        return halo_copy(
            own.at[c], rows_at(c, HB - share * by), shifted(by), halo_send.at[c, n], halo_recv.at[c, n]
        )

    def far_copy(c, n):
        by = 1 - 2 * n
        source, target = rows_at(c, HB - share * by), rows_at(c, HB - 2 * share * by)
        return halo_copy(source, target, shifted(by), halo_send.at[c, 2 + n], halo_recv.at[c, 2 + n])

    def to_relay(c, n):
        by = 1 - 2 * n
        across = r, t - (SPAN - 1) * by
        source = rows_at(c, HB - share * by)
        return halo_copy(source, relay.at[c], across, halo_send.at[c, 2 + n], relay_recv.at[c])

    def from_relay(c, n):
        by = 1 - 2 * n
        target = rows_at(c, HB - 2 * share * by)
        return halo_copy(relay.at[c], target, shifted(SPAN * by), relay_send.at[c], halo_recv.at[c, 2 + n])

    def skip_copy(n):
        by = 1 - 2 * n
        c = CHUNKS - 1
        target = rows_at(c, HB - 2 * share * by)
        return halo_copy(own.at[c], target, shifted(2 * by), skip_send, halo_recv.at[c, 2 + n])

    turning, late, skips = (last, first), (first, last), (place == SPAN - 2, place == 1)
    ahead, behind = (within(1), within(-1)), (within(-1), within(1))
    skips = tuple(skips[n] & within(2 - 4 * n) for n in range(2))
    relaying = tuple(late[n] & within(SPAN * (1 - 2 * n)) for n in range(2))
    far_on = tuple(jnp.logical_not(turning[n]) & behind[n] & ahead[n] for n in range(2))
    relay_on = tuple(turning[n] & ahead[n] for n in range(2))

    def pass_fast(c):
        for n in range(2):

            @pl.when(jnp.logical_not(late[n]))
            def _():
                near_copy(c, n).wait_recv()

                @pl.when(far_on[n])
                def _():
                    far_copy(c, n).start()

                if c < CHUNKS - 1:

                    @pl.when(relay_on[n])
                    def _():
                        to_relay(c, n).start()

    def pass_late(c):
        for n in range(2):

            @pl.when(late[n] & behind[n])
            def _():
                near_copy(c, n).wait_recv()

                @pl.when(far_on[n])
                def _():
                    far_copy(c, n).start()

    def pass_relay(c):
        for n in range(2):

            @pl.when(relaying[n])
            def _():
                to_relay(c, n).wait_recv()
                from_relay(c, n).start()

    for c in range(CHUNKS - 1):
        for n in range(2):

            @pl.when(ahead[n])
            def _():
                near_copy(c, n).start()

    for n in range(2):

        @pl.when(skips[n])
        def _():
            skip_copy(n).start()

        @pl.when(jnp.logical_not(turning[n]) & ahead[n])
        def _():
            near_copy(CHUNKS - 1, n).start()

    for load in loads[2:]:
        load.wait()
    edge = (t < 2) | (t >= cols_n - 2)
    total_rows = rows_n * RB
    count = count_s[0, 0]
    picks = []
    for s in range(slots):
        column = cols_s[0, s]
        row = (r - 1) * RB + column
        live = (count > s) & (row >= 0) & (row < total_rows)
        centre = (column >= RB) & (column < 2 * RB)
        picks.append(jnp.clip(column - RB - t * share + HB, 0, halo0.shape[0] - 1))
        line = jnp.clip(rows_s[0, s] - t * share, 0, share - 1)
        for c in range(CHUNKS):
            value = own[c, line]
            zero = jnp.zeros_like(value)
            stack[c, s * size : (s + 1) * size, :] = jnp.where(live & centre, value, zero)

    def turn(into):
        flips = [stack[c].T for c in range(CHUNKS)]
        into[0:LANES, :] = flips[0]
        into[LANES:size, :] = flips[2][:half]
        into[size : size + LANES, :] = flips[1]
        into[size + LANES :, :] = flips[2][half:]

    turn(left)
    pass_fast(0)
    pass_fast(1)
    for n in range(2):

        @pl.when(relay_on[n])
        def _():
            near_copy(CHUNKS - 1, n).start()

    pass_relay(0)
    pass_fast(2)
    pass_relay(1)

    @pl.when(edge)
    def _():
        for s in range(slots):
            column = cols_s[0, s]
            row = (r - 1) * RB + column
            live = (count > s) & (row >= 0) & (row < total_rows)
            outside = (column < RB) | (column >= 2 * RB)
            line = jnp.clip(rows_s[0, s] - t * share, 0, share - 1)
            for c in range(CHUNKS):
                value = own[c, line]
                zero = jnp.zeros_like(value)
                stack[c, s * size : (s + 1) * size, :] = jnp.where(live & outside, value, zero)
        turn(side_left)

    def pieces(value):
        value = value.reshape(lines, SPAN, piece, LANES)
        value = jnp.stack([value[:, k] for k in range(SPAN)])
        return value.reshape(SPAN, lines * piece, LANES).astype(mine.dtype)

    def band_copy(c, by):
        device = beside(by)
        return pltpu.make_async_remote_copy(
            src_ref=mine.at[c, lax.rem(place + by, SPAN)],
            dst_ref=gots[c].at[place],
            send_sem=band_send.at[c],
            recv_sem=band_recv.at[c],
            device_id=device,
            device_id_type=MESH,
        )

    def side_copy(c, by):
        return pltpu.make_async_remote_copy(
            src_ref=side_mine.at[c, lax.rem(place + by, SPAN)],
            dst_ref=side_gots[c].at[lax.rem(t, 2)],
            send_sem=side_send.at[c],
            recv_sem=side_recv.at[c],
            device_id=beside(by),
            device_id_type=MESH,
        )

    def line_copy(c, by):
        return pltpu.make_async_remote_copy(
            src_ref=part.at[c, lax.rem(line_of + by, lines)],
            dst_ref=lined[c].at[line_of],
            send_sem=line_send.at[c],
            recv_sem=line_recv.at[c],
            device_id=above(by),
            device_id_type=MESH,
        )

    def side_line_copy(c, by):
        return pltpu.make_async_remote_copy(
            src_ref=side_part.at[c, lax.rem(line_of + by, lines)],
            dst_ref=side_lined[c].at[line_of // (lines - 1)],
            send_sem=side_line_send.at[c],
            recv_sem=side_line_recv.at[c, line_of // (lines - 1)],
            device_id=above(by),
            device_id_type=MESH,
        )

    def landed(ref, count, sem):
        some = ref.at[pl.ds(0, count)]
        pltpu.make_async_copy(some, some, sem).wait()

    outer = (line_of == 0) | (line_of == lines - 1)

    def work(c):
        for n in range(2):

            @pl.when(within(4 * n - 2))
            def _():
                far_copy(c, n).wait_recv()

        for s in range(slots):
            value = jnp.dot(a_buf[s], halos[c][picks[s]], preferred_element_type=jnp.float32)
            prod[s * size : (s + 1) * size, :] = value.astype(prod.dtype)
        mine[c] = pieces(jnp.dot(left[...], prod[...], preferred_element_type=jnp.float32))
        for by in range(1, SPAN):
            band_copy(c, by).start()
        gots[c][place] = mine[c, place]

        @pl.when(edge)
        def _():
            side_mine[c] = pieces(jnp.dot(side_left[...], prod[...], preferred_element_type=jnp.float32))
            for by in range(1, SPAN):
                side_copy(c, by).start()
            side_gots[c][lax.rem(t, 2)] = side_mine[c, place]

    def hand_on(c):
        landed(gots[c], SPAN - 1, band_recv.at[c])
        total = jnp.sum(gots[c][...].astype(jnp.float32), axis=0).reshape(lines, piece, LANES)
        part[c] = total
        for by in range(1, lines):
            line_copy(c, by).start()
        lined[c][line_of] = part[c, line_of]

        @pl.when(outer)
        def _():
            @pl.when(edge)
            def _():
                landed(side_gots[c], 1, side_recv.at[c])

            @pl.when(jnp.logical_not(edge))
            def _():
                landed(side_gots[c], 2, side_recv.at[c])

            sides = side_gots[c][...].astype(jnp.float32)
            side_part[c] = (sides[0] + sides[1]).reshape(lines, piece, LANES)
            for by in range(1, lines):
                side_line_copy(c, by).start()
            side_lined[c][line_of // (lines - 1)] = side_part[c, line_of]

    pass_late(0)
    pass_late(1)
    work(0)
    pass_late(2)
    work(1)
    hand_on(0)
    work(2)
    hand_on(1)
    hand_on(2)
    for c in range(CHUNKS):
        for n in range(2):

            @pl.when(ahead[n])
            def _():
                near_copy(c, n).wait_send()

            @pl.when(far_on[n])
            def _():
                far_copy(c, n).wait_send()

            if c < CHUNKS - 1:

                @pl.when(relay_on[n])
                def _():
                    to_relay(c, n).wait_send()

                @pl.when(relaying[n])
                def _():
                    from_relay(c, n).wait_send()

            else:

                @pl.when(skips[n])
                def _():
                    skip_copy(n).wait_send()

    sums = []
    for c in range(CHUNKS):
        landed(lined[c], lines - 1, line_recv.at[c])
        for k in range(2):

            @pl.when(line_of != k * (lines - 1))
            def _():
                landed(side_lined[c], 1, side_line_recv.at[c, k])

        sums.append((side_lined[c][0], jnp.sum(lined[c][...], axis=0), side_lined[c][1]))

    for c in range(CHUNKS):
        landed(mine.at[c], SPAN - 1, band_send.at[c])
        landed(part.at[c], lines - 1, line_send.at[c])

        @pl.when(edge)
        def _():
            landed(side_mine.at[c], SPAN - 1, side_send.at[c])

        @pl.when(outer)
        def _():
            landed(side_part.at[c], lines - 1, side_line_send.at[c])

    blocks = []
    for j in range(3):
        low, high, mixed = sums[0][j], sums[1][j], sums[2][j]
        blocks += [low, mixed[:, :half], high, mixed[:, half:]]
    empty = jnp.zeros((piece, size), jnp.float32)

    @pl.when(t < cols_n // CR)
    def _():
        out_ref[...] = jnp.concatenate([empty] + blocks, axis=1)

    @pl.when(t >= cols_n // CR)
    def _():
        out_ref[...] = jnp.concatenate(blocks + [empty], axis=1)


def local(a_vals, a_rows, a_cols, a_count, p_vals, p_cols):
    slots, size = a_vals.shape[1], a_vals.shape[2]
    share = p_vals.shape[0]
    cols_n = lax.axis_size("col")
    piece = CR * size // cols_n
    lines = cols_n // SPAN
    width = share + 2 * HB
    kind = p_vals.dtype
    anywhere = pl.BlockSpec(memory_space=pltpu.HBM)
    halo = pltpu.VMEM((width, size, LANES), kind)
    got = pltpu.VMEM((SPAN, lines * piece, LANES), kind)
    side_got = pltpu.VMEM((2, lines * piece, LANES), kind)
    lined = pltpu.VMEM((lines, piece, LANES), jnp.float32)
    side_lined = pltpu.VMEM((2, piece, LANES), jnp.float32)
    return pl.pallas_call(
        kernel,
        out_shape=jax.ShapeDtypeStruct((piece, 7 * size), jnp.float32),
        in_specs=[anywhere] * 6,
        out_specs=pl.BlockSpec(memory_space=pltpu.VMEM),
        scratch_shapes=[
            pltpu.VMEM((slots, size, size), kind),
            pltpu.VMEM((share, 2, size, size), kind),
            pltpu.SMEM((1, slots), jnp.int32),
            pltpu.SMEM((1, slots), jnp.int32),
            pltpu.SMEM((1, 1), jnp.int32),
            pltpu.SMEM((2, LANES), jnp.int32),
            pltpu.VMEM((CHUNKS, share, size, LANES), kind),
            halo, halo, halo,
            pltpu.VMEM((CHUNKS, share, size, LANES), kind),
            pltpu.VMEM((CHUNKS, slots * size, LANES), kind),
            pltpu.VMEM((CR * size, slots * size), kind),
            pltpu.VMEM((CR * size, slots * size), kind),
            pltpu.VMEM((slots * size, LANES), kind),
            pltpu.VMEM((CHUNKS, SPAN, lines * piece, LANES), kind),
            got, got, got,
            pltpu.VMEM((CHUNKS, SPAN, lines * piece, LANES), kind),
            side_got, side_got, side_got,
            pltpu.VMEM((CHUNKS, lines, piece, LANES), jnp.float32),
            lined, lined, lined,
            pltpu.VMEM((CHUNKS, lines, piece, LANES), jnp.float32),
            side_lined, side_lined, side_lined,
            pltpu.SemaphoreType.DMA((6,)),
            pltpu.SemaphoreType.DMA((CHUNKS, 4)),
            pltpu.SemaphoreType.DMA((CHUNKS, 4)),
            pltpu.SemaphoreType.DMA((CHUNKS,)),
            pltpu.SemaphoreType.DMA((CHUNKS,)),
            pltpu.SemaphoreType.DMA,
        ]
        + [pltpu.SemaphoreType.DMA((CHUNKS,))] * 7
        + [pltpu.SemaphoreType.DMA((CHUNKS, 2))],
        compiler_params=pltpu.CompilerParams(
            collective_id=0, has_side_effects=True, vmem_limit_bytes=62 * 2**20
        ),
        name="galerkin",
    )(a_vals, a_rows, a_cols, a_count, p_vals, p_cols.T)


def solution(mesh):
    placed = (
        P("row", "col", None, None),
        P("row", "col"),
        P("row", "col"),
        P("row", "col"),
        P(("row", "col"), None, None, None),
        P(),
    )
    return jax.shard_map(
        local, mesh=mesh, in_specs=placed, out_specs=P(("row", "col"), None), check_vma=False
    )
```

```python
import functools

import jax
import jax.numpy as jnp
from jax import lax
from jax.experimental import pallas as pl
from jax.experimental.pallas import tpu as pltpu
from jax.sharding import PartitionSpec as P

HB = 4
RB = 32
CR = 2
LANES = 128
CHUNKS = 3
MESH = pl.DeviceIdType.MESH
SPAN = 4


def kernel(
    a_hbm, rows_hbm, cols_hbm, count_hbm, p_hbm, pc_hbm, out_ref,
    a_buf, p_buf, rows_s, cols_s, count_s, pc_s,
    own, halo0, halo1, halo2, stack, left, side_left, prod,
    mine, got0, got1, got2, side_mine, side_got0, side_got1, side_got2,
    part, lined0, lined1, lined2, side_part, side_lined0, side_lined1, side_lined2,
    load_sem, halo_send, halo_recv, skip_send,
    band_send, band_recv, side_send, side_recv, line_send, line_recv, side_line_send, side_line_recv,
):
    rows_n, cols_n = lax.axis_size("row"), lax.axis_size("col")
    r, t = lax.axis_index("row"), lax.axis_index("col")
    slots, size = a_buf.shape[0], a_buf.shape[1]
    share = p_buf.shape[0]
    half = size - LANES
    piece = CR * size // cols_n
    lined, side_lined = (lined0, lined1, lined2), (side_lined0, side_lined1, side_lined2)
    halos, gots, side_gots = (halo0, halo1, halo2), (got0, got1, got2), (side_got0, side_got1, side_got2)
    first_row = r * RB + t * share
    aligned = pl.multiple_of(first_row // LANES * LANES, LANES)

    flat = r * cols_n + t
    tiles = rows_n * cols_n

    def within(by):
        return (flat + by >= 0) & (flat + by < tiles)

    def shifted(by):
        other = lax.rem(flat + by + tiles, tiles)
        return other // cols_n, lax.rem(other, cols_n)

    lines = cols_n // SPAN
    place, line_of = lax.rem(t, SPAN), t // SPAN
    first, last = place == 0, place == SPAN - 1

    def beside(by):
        return r, line_of * SPAN + lax.rem(place + by, SPAN)

    def above(by):
        return r, lax.rem(t + by * SPAN, cols_n)

    loads = [
        pltpu.make_async_copy(p_hbm, p_buf, load_sem.at[0]),
        pltpu.make_async_copy(pc_hbm.at[:, pl.ds(aligned, LANES)], pc_s, load_sem.at[1]),
        pltpu.make_async_copy(a_hbm.at[0], a_buf, load_sem.at[2]),
        pltpu.make_async_copy(rows_hbm, rows_s, load_sem.at[3]),
        pltpu.make_async_copy(cols_hbm, cols_s, load_sem.at[4]),
        pltpu.make_async_copy(count_hbm, count_s, load_sem.at[5]),
    ]
    for load in loads:
        load.start()

    barrier = pltpu.get_barrier_semaphore()
    friends = [beside(by) for by in range(1, SPAN)] + [above(by) for by in range(1, lines)]
    for friend in friends:
        pl.semaphore_signal(barrier, inc=1, device_id=friend, device_id_type=MESH)
    expected = jnp.int32(len(friends))
    for by in (1, -1, 2, -2):
        expected += within(by).astype(jnp.int32)

        @pl.when(within(by))
        def _():
            pl.semaphore_signal(barrier, inc=1, device_id=shifted(by), device_id_type=MESH)

    loads[0].wait()
    loads[1].wait()
    for k in range(share):
        swap = jnp.clip(pc_s[0, first_row - aligned + k], 0, 1)
        low = p_buf[k, swap]
        high = p_buf[k, 1 - swap]
        parts = (low[:, :LANES], high[:, :LANES], jnp.concatenate([low[:, LANES:], high[:, LANES:]], axis=1))
        for c in range(CHUNKS):
            own[c, k] = parts[c]
            halos[c][HB + k] = parts[c]

    for n in range(2):
        by = 1 - 2 * n
        for far in (1, 2):

            @pl.when(jnp.logical_not(within(-far * by)))
            def _():
                for c in range(CHUNKS):
                    empty_rows = jnp.zeros((share, size, LANES), halos[c].dtype)
                    halos[c][HB - far * share * by : HB - far * share * by + share] = empty_rows

    for load in loads[2:]:
        load.wait()
    has = (r > 0, r < rows_n - 1)
    edge = ((t < 2) & has[0]) | ((t >= cols_n - 2) & has[1])
    outer = ((line_of == 0) & has[0]) | ((line_of == lines - 1) & has[1])
    count = count_s[0, 0]
    columns = [cols_s[0, s] for s in range(slots)]
    picks = [jnp.clip(column - RB - t * share + HB, 0, halo0.shape[0] - 1) for column in columns]

    def fill(centre):
        for s in range(slots):
            row = (r - 1) * RB + columns[s]
            live = (count > s) & (row >= 0) & (row < rows_n * RB)
            inside = (columns[s] >= RB) & (columns[s] < 2 * RB)
            kept = live & (inside if centre else jnp.logical_not(inside))
            line = jnp.clip(rows_s[0, s] - t * share, 0, share - 1)
            for c in range(CHUNKS):
                value = own[c, line]
                stack[c, s * size : (s + 1) * size, :] = jnp.where(kept, value, jnp.zeros_like(value))

    def turn(into):
        flips = [stack[c].T for c in range(CHUNKS)]
        into[0:LANES, :] = flips[0]
        into[LANES:size, :] = flips[2][:half]
        into[size : size + LANES, :] = flips[1]
        into[size + LANES :, :] = flips[2][half:]

    @pl.when(edge)
    def _():
        fill(False)
        turn(side_left)

    for k in range(2):

        @pl.when(jnp.logical_not(has[k]))
        def _():
            for c in range(CHUNKS):
                side_lined[c][k] = jnp.zeros((piece, LANES), jnp.float32)

    pl.semaphore_wait(barrier, expected)

    def halo_copy(source, target, device, sent, landed):
        return pltpu.make_async_remote_copy(
            src_ref=source,
            dst_ref=target,
            send_sem=sent,
            recv_sem=landed,
            device_id=device,
            device_id_type=MESH,
        )

    def rows_at(c, start):
        return halos[c].at[pl.ds(start, share)]

    def near_copy(c, n):
        by = 1 - 2 * n
        return halo_copy(
            own.at[c], rows_at(c, HB - share * by), shifted(by), halo_send.at[c, n], halo_recv.at[c, n]
        )

    def far_copy(c, n):
        by = 1 - 2 * n
        source, target = rows_at(c, HB - share * by), rows_at(c, HB - 2 * share * by)
        return halo_copy(source, target, shifted(by), halo_send.at[c, 2 + n], halo_recv.at[c, 2 + n])

    def skip_copy(c, n):
        by = 1 - 2 * n
        target = rows_at(c, HB - 2 * share * by)
        return halo_copy(own.at[c], target, shifted(2 * by), skip_send.at[c], halo_recv.at[c, 2 + n])

    turning, late, skips = (last, first), (first, last), (place == SPAN - 2, place == 1)
    ahead, behind = (within(1), within(-1)), (within(-1), within(1))
    skips = tuple(skips[n] & within(2 - 4 * n) for n in range(2))
    far_on = tuple(jnp.logical_not(turning[n]) & behind[n] & ahead[n] for n in range(2))

    def pass_fast(c):
        for n in range(2):

            @pl.when(jnp.logical_not(late[n]))
            def _():
                near_copy(c, n).wait_recv()

                @pl.when(far_on[n])
                def _():
                    far_copy(c, n).start()

    def pass_late(c):
        for n in range(2):

            @pl.when(late[n] & behind[n])
            def _():
                near_copy(c, n).wait_recv()

                @pl.when(far_on[n])
                def _():
                    far_copy(c, n).start()

    def start_near(c, quick):
        for n in range(2):

            @pl.when(ahead[n] & (jnp.logical_not(turning[n]) if quick else turning[n]))
            def _():
                near_copy(c, n).start()

    for c in range(CHUNKS - 1):
        start_near(c, True)
        start_near(c, False)
    for c in range(CHUNKS):
        for n in range(2):

            @pl.when(skips[n])
            def _():
                skip_copy(c, n).start()

    start_near(CHUNKS - 1, True)
    fill(True)
    pass_fast(0)
    turn(left)
    pass_fast(1)
    start_near(2, False)
    pass_fast(2)

    def pieces(value):
        value = value.reshape(lines, SPAN, piece, LANES)
        value = jnp.stack([value[:, k] for k in range(SPAN)])
        return value.reshape(SPAN, lines * piece, LANES).astype(mine.dtype)

    def band_copy(c, by):
        device = beside(by)
        return pltpu.make_async_remote_copy(
            src_ref=mine.at[c, lax.rem(place + by, SPAN)],
            dst_ref=gots[c].at[place],
            send_sem=band_send.at[c],
            recv_sem=band_recv.at[c],
            device_id=device,
            device_id_type=MESH,
        )

    def side_copy(c, by):
        return pltpu.make_async_remote_copy(
            src_ref=side_mine.at[c, lax.rem(place + by, SPAN)],
            dst_ref=side_gots[c].at[lax.rem(t, 2)],
            send_sem=side_send.at[c],
            recv_sem=side_recv.at[c],
            device_id=beside(by),
            device_id_type=MESH,
        )

    def line_copy(c, by):
        return pltpu.make_async_remote_copy(
            src_ref=part.at[c, lax.rem(line_of + by, lines)],
            dst_ref=lined[c].at[line_of],
            send_sem=line_send.at[c],
            recv_sem=line_recv.at[c],
            device_id=above(by),
            device_id_type=MESH,
        )

    def side_line_copy(c, by):
        return pltpu.make_async_remote_copy(
            src_ref=side_part.at[c, lax.rem(line_of + by, lines)],
            dst_ref=side_lined[c].at[line_of // (lines - 1)],
            send_sem=side_line_send.at[c],
            recv_sem=side_line_recv.at[c, line_of // (lines - 1)],
            device_id=above(by),
            device_id_type=MESH,
        )

    def landed(ref, count, sem):
        some = ref.at[pl.ds(0, count)]
        pltpu.make_async_copy(some, some, sem).wait()

    def work(c):
        for n in range(2):

            @pl.when(within(4 * n - 2))
            def _():
                far_copy(c, n).wait_recv()

        for s in range(slots):
            value = jnp.dot(a_buf[s], halos[c][picks[s]], preferred_element_type=jnp.float32)
            prod[s * size : (s + 1) * size, :] = value.astype(prod.dtype)
        mine[c] = pieces(jnp.dot(left[...], prod[...], preferred_element_type=jnp.float32))
        for by in range(1, SPAN):
            band_copy(c, by).start()
        gots[c][place] = mine[c, place]

        @pl.when(edge)
        def _():
            side_mine[c] = pieces(jnp.dot(side_left[...], prod[...], preferred_element_type=jnp.float32))
            for by in range(1, SPAN):
                side_copy(c, by).start()
            side_gots[c][lax.rem(t, 2)] = side_mine[c, place]

    def hand_on(c):
        landed(gots[c], SPAN - 1, band_recv.at[c])
        total = jnp.sum(gots[c][...].astype(jnp.float32), axis=0).reshape(lines, piece, LANES)
        part[c] = total
        for by in range(1, lines):
            line_copy(c, by).start()
        lined[c][line_of] = part[c, line_of]

        @pl.when(outer)
        def _():
            @pl.when(edge)
            def _():
                landed(side_gots[c], 1, side_recv.at[c])

            @pl.when(jnp.logical_not(edge))
            def _():
                landed(side_gots[c], 2, side_recv.at[c])

            sides = side_gots[c][...].astype(jnp.float32)
            side_part[c] = (sides[0] + sides[1]).reshape(lines, piece, LANES)
            for by in range(1, lines):
                side_line_copy(c, by).start()
            side_lined[c][line_of // (lines - 1)] = side_part[c, line_of]

    pass_late(0)
    pass_late(1)
    work(0)
    pass_late(2)
    work(1)
    hand_on(0)
    work(2)
    hand_on(1)
    hand_on(2)
    for c in range(CHUNKS):
        for n in range(2):

            @pl.when(ahead[n])
            def _():
                near_copy(c, n).wait_send()

            @pl.when(far_on[n])
            def _():
                far_copy(c, n).wait_send()

            @pl.when(skips[n])
            def _():
                skip_copy(c, n).wait_send()

    sums = []
    for c in range(CHUNKS):
        landed(lined[c], lines - 1, line_recv.at[c])
        for k in range(2):

            @pl.when((line_of != k * (lines - 1)) & has[k])
            def _():
                landed(side_lined[c], 1, side_line_recv.at[c, k])

        sums.append((side_lined[c][0], jnp.sum(lined[c][...], axis=0), side_lined[c][1]))

    for c in range(CHUNKS):
        landed(mine.at[c], SPAN - 1, band_send.at[c])
        landed(part.at[c], lines - 1, line_send.at[c])

        @pl.when(edge)
        def _():
            landed(side_mine.at[c], SPAN - 1, side_send.at[c])

        @pl.when(outer)
        def _():
            landed(side_part.at[c], lines - 1, side_line_send.at[c])

    blocks = []
    for j in range(3):
        low, high, mixed = sums[0][j], sums[1][j], sums[2][j]
        blocks += [low, mixed[:, :half], high, mixed[:, half:]]
    empty = jnp.zeros((piece, size), jnp.float32)

    @pl.when(t < cols_n // CR)
    def _():
        out_ref[...] = jnp.concatenate([empty] + blocks, axis=1)

    @pl.when(t >= cols_n // CR)
    def _():
        out_ref[...] = jnp.concatenate(blocks + [empty], axis=1)


def local(a_vals, a_rows, a_cols, a_count, p_vals, p_cols):
    slots, size = a_vals.shape[1], a_vals.shape[2]
    share = p_vals.shape[0]
    cols_n = lax.axis_size("col")
    piece = CR * size // cols_n
    lines = cols_n // SPAN
    width = share + 2 * HB
    kind = p_vals.dtype
    anywhere = pl.BlockSpec(memory_space=pltpu.HBM)
    halo = pltpu.VMEM((width, size, LANES), kind)
    got = pltpu.VMEM((SPAN, lines * piece, LANES), kind)
    side_got = pltpu.VMEM((2, lines * piece, LANES), kind)
    lined = pltpu.VMEM((lines, piece, LANES), jnp.float32)
    side_lined = pltpu.VMEM((2, piece, LANES), jnp.float32)
    return pl.pallas_call(
        kernel,
        out_shape=jax.ShapeDtypeStruct((piece, 7 * size), jnp.float32),
        in_specs=[anywhere] * 6,
        out_specs=pl.BlockSpec(memory_space=pltpu.VMEM),
        scratch_shapes=[
            pltpu.VMEM((slots, size, size), kind),
            pltpu.VMEM((share, 2, size, size), kind),
            pltpu.SMEM((1, slots), jnp.int32),
            pltpu.SMEM((1, slots), jnp.int32),
            pltpu.SMEM((1, 1), jnp.int32),
            pltpu.SMEM((2, LANES), jnp.int32),
            pltpu.VMEM((CHUNKS, share, size, LANES), kind),
            halo, halo, halo,
            pltpu.VMEM((CHUNKS, slots * size, LANES), kind),
            pltpu.VMEM((CR * size, slots * size), kind),
            pltpu.VMEM((CR * size, slots * size), kind),
            pltpu.VMEM((slots * size, LANES), kind),
            pltpu.VMEM((CHUNKS, SPAN, lines * piece, LANES), kind),
            got, got, got,
            pltpu.VMEM((CHUNKS, SPAN, lines * piece, LANES), kind),
            side_got, side_got, side_got,
            pltpu.VMEM((CHUNKS, lines, piece, LANES), jnp.float32),
            lined, lined, lined,
            pltpu.VMEM((CHUNKS, lines, piece, LANES), jnp.float32),
            side_lined, side_lined, side_lined,
            pltpu.SemaphoreType.DMA((6,)),
            pltpu.SemaphoreType.DMA((CHUNKS, 4)),
            pltpu.SemaphoreType.DMA((CHUNKS, 4)),
            pltpu.SemaphoreType.DMA((CHUNKS,)),
        ]
        + [pltpu.SemaphoreType.DMA((CHUNKS,))] * 7
        + [pltpu.SemaphoreType.DMA((CHUNKS, 2))],
        compiler_params=pltpu.CompilerParams(
            collective_id=0, has_side_effects=True, vmem_limit_bytes=62 * 2**20
        ),
        name="galerkin",
    )(a_vals, a_rows, a_cols, a_count, p_vals, p_cols.T)


def solution(mesh):
    placed = (
        P("row", "col", None, None),
        P("row", "col"),
        P("row", "col"),
        P("row", "col"),
        P(("row", "col"), None, None, None),
        P(),
    )
    return jax.shard_map(
        local, mesh=mesh, in_specs=placed, out_specs=P(("row", "col"), None), check_vma=False
    )
```
